32 devices in a mesh: groups: 2 (over x), lon: 16 (over z, y, core).
Axes of the slice: x: 2, y: 2, z: 4, core: 2. Of those that a mesh axis runs over, the one named last changes fastest.
Arguments:
- queries: bfloat16 [8192, 1024], P(('groups', 'lon')), parts along dimension 0, may hold values from -8 to 8
- key_tokens: bfloat16 [8192, 1024], P(('groups', 'lon')), parts along dimension 0, may hold values from -8 to 8
- value_tokens: bfloat16 [8192, 1024], P(('groups', 'lon')), parts along dimension 0, may hold values from -6 to 6
- grad_out: bfloat16 [8192, 1024], P(('groups', 'lon')), parts along dimension 0, may hold values from -6 to 6
- out_weight: bfloat16 [1024, 1024], replicated, may hold values from -3 to 3
- pattern: int32 [32, 3], replicated, may hold values from 0 to 31, as said below
- valid_rows: int32 [32], replicated, may hold values from 64 to 128, as said below
Outputs:
- layer_out: bfloat16 [8192, 1024], P(('groups', 'lon')), parts along dimension 0
- grad_queries: bfloat16 [8192, 1024], P(('groups', 'lon')), parts along dimension 0
- grad_keys: bfloat16 [8192, 1024], P(('groups', 'lon')), parts along dimension 0
- grad_values: bfloat16 [8192, 1024], P(('groups', 'lon')), parts along dimension 0
The draws below stay inside these ranges and needn't reach their ends.
There are 2 independent parts, one for each index of `groups`. The reference program is written for one: setup_inputs(seed, part) draws one part's arguments, and reference() takes and returns one part's arrays. A program takes and returns all parts, laid end to end along the dimension named above; an argument that names none is the same for every part. Nothing has to cross between parts.
Inputs may be any that keep to these rules, and one draw needn't show every extreme that they name: `pattern`: block g lies in longitude strip g // 2 at latitude index g % 2. Row g names three key blocks: column 1 is g itself, column 0 a block of strip (g // 2 - 1) mod 16, column 2 a block of strip (g // 2 + 1) mod 16, each at a latitude index that differs from g's by at most one. The first valid_rows[g] tokens of block g are live, the others are padding.
All inputs are finite; a program needn't handle non-finite values.
Results may differ from the reference program's by a relative error of at most 0.028.
Values may be sent and summed in bfloat16 or wider, within the bound.
A program may use at most 128 MiB of HBM per device.

```python
import jax
import jax.numpy as jnp
from jax import lax

D = 1024
HEADS = 16
TILE = 128
BLK_DEV = 2
N_BLOCKS = 32
TOKENS = 4096
N_LON = 16


def draw_queries(key, part):
    return jnp.clip(jax.random.normal(jax.random.fold_in(key, 11), (TOKENS, D)), -6.0, 6.0).astype(jnp.bfloat16)


def draw_key_tokens(key, part):
    return jnp.clip(jax.random.normal(jax.random.fold_in(key, 21), (TOKENS, D)), -6.0, 6.0).astype(jnp.bfloat16)


def draw_pattern(key, part):
    block_index = jnp.arange(N_BLOCKS, dtype=jnp.int32)
    strip_index = block_index // BLK_DEV
    latitude = block_index % BLK_DEV
    west_step = jax.random.randint(jax.random.fold_in(key, 31), (N_BLOCKS,), -1, 2)
    east_step = jax.random.randint(jax.random.fold_in(key, 32), (N_BLOCKS,), -1, 2)
    west_lat = jnp.clip(latitude + west_step, 0, BLK_DEV - 1)
    east_lat = jnp.clip(latitude + east_step, 0, BLK_DEV - 1)
    west_block = (strip_index - 1) % N_LON * BLK_DEV + west_lat
    east_block = (strip_index + 1) % N_LON * BLK_DEV + east_lat
    return jnp.stack((west_block, block_index, east_block), axis=1).astype(jnp.int32)


def draw_valid_rows(key, part):
    counts = jax.random.randint(jax.random.fold_in(key, 41), (N_BLOCKS,), TILE // 2, TILE + 1)
    return counts.at[0].set(TILE // 2).at[1].set(TILE).astype(jnp.int32)


def block_scale(stream_key, shape, split, smallest, high):
    def one(dim, blocks):
        steps = jax.random.uniform(jax.random.fold_in(jax.random.fold_in(stream_key, 6), dim), (blocks,), jnp.float32, smallest / len(split), high / len(split))
        return jnp.repeat(jnp.exp(steps), shape[dim] // blocks).reshape((-1,) + (1,) * (len(shape) - dim - 1))

    factor_of = one(*split[0])
    for cut in split[1:]:
        factor_of = factor_of * one(*cut)
    return factor_of


def scatter_about(key, shape, deviation, reach, pieces=(), kind=jnp.bfloat16):
    result = deviation * jax.random.normal(key, shape, jnp.float32)
    if pieces:
        result = result * block_scale(key, shape, pieces, -0.22, 0.18)
    return jnp.clip(result, -reach, reach).astype(kind)


def setup_inputs(seed: int = 0, part: int = 0) -> dict:
    key_list = jax.random.split(jax.random.key(seed), 8)
    part_splits = jax.random.split(jax.random.fold_in(key_list[7], part), 8)
    queries = draw_queries(jax.random.fold_in(jax.random.fold_in(key_list[7], part), 71), part)
    key_tokens = draw_key_tokens(jax.random.fold_in(jax.random.fold_in(key_list[7], part), 71), part)
    value_tokens = scatter_about(part_splits[2], (TOKENS, D), 1.0, 6.0, ((0, 16),))
    grad_out = scatter_about(part_splits[3], (TOKENS, D), 1.0, 6.0, ((0, 16),))
    out_weight = scatter_about(key_list[4], (D, D), (max(D // 256, 1)) ** -0.5, 3.0)
    pattern = draw_pattern(jax.random.fold_in(key_list[7], 71), part)
    valid_rows = draw_valid_rows(jax.random.fold_in(key_list[7], 71), part)
    return dict(queries=queries, key_tokens=key_tokens, value_tokens=value_tokens, grad_out=grad_out, out_weight=out_weight, pattern=pattern, valid_rows=valid_rows)


def reference(queries, key_tokens, value_tokens, grad_out, out_weight, pattern, valid_rows):
    features = queries.shape[1]
    head_size = features // HEADS
    score_scale = head_size ** (-0.5)
    near_span = 3 * TILE
    live_mask = jnp.arange(TILE, dtype=jnp.int32)[None, :] < valid_rows[:, None]
    live_float = live_mask.astype(jnp.float32)
    root_counts = jnp.sqrt(valid_rows.astype(jnp.float32))
    key_blocks = key_tokens.reshape(N_BLOCKS, TILE, features)
    value_blocks = value_tokens.reshape(N_BLOCKS, TILE, features)
    pooled_keys = jnp.einsum('gt,gtd->gd', live_float, key_blocks.astype(jnp.float32))
    pooled_values = jnp.einsum('gt,gtd->gd', live_float, value_blocks.astype(jnp.float32))
    summary_keys = (pooled_keys / root_counts[:, None]).astype(jnp.bfloat16)
    summary_values = (pooled_values / root_counts[:, None]).astype(jnp.bfloat16)
    grad_attended = jnp.dot(grad_out, out_weight.T, preferred_element_type=jnp.float32).astype(jnp.bfloat16)
    far_keys = summary_keys.astype(jnp.float32).reshape(N_BLOCKS, HEADS, head_size)
    far_values = summary_values.astype(jnp.float32).reshape(N_BLOCKS, HEADS, head_size)
    far_live = jnp.ones((N_BLOCKS,), dtype=bool)
    query_all = queries.reshape(N_BLOCKS, TILE, HEADS, head_size)
    grad_all = grad_attended.reshape(N_BLOCKS, TILE, HEADS, head_size)

    def one_block(carried, inputs):
        far_grad_keys, far_grad_values = carried
        query_block, grad_block, block_ids = inputs
        near_keys = key_blocks[block_ids].reshape(near_span, HEADS, head_size).astype(jnp.float32)
        near_values = value_blocks[block_ids].reshape(near_span, HEADS, head_size).astype(jnp.float32)
        key_all = jnp.concatenate((near_keys, far_keys), axis=0)
        value_all = jnp.concatenate((near_values, far_values), axis=0)
        mask_all = jnp.concatenate((live_mask[block_ids].reshape(near_span), far_live), axis=0)
        query_float = query_block.astype(jnp.float32)
        scores = jnp.einsum('thc,lhc->htl', query_float, key_all) * score_scale
        scores = jnp.where(mask_all[None, None, :], scores, -jnp.inf)
        row_top = lax.optimization_barrier(jnp.max(scores, axis=-1, keepdims=True))
        log_total = row_top[..., 0] + jnp.log(lax.optimization_barrier(jnp.sum(jnp.exp(scores - row_top), axis=-1)))
        chances = jnp.exp(scores - log_total[..., None])
        rounded = lax.optimization_barrier(chances.astype(jnp.bfloat16)).astype(jnp.float32)
        attended = lax.optimization_barrier(jnp.einsum('htl,lhc->thc', rounded, value_all).astype(jnp.bfloat16))
        grad_float = grad_block.astype(jnp.float32)
        row_delta = jnp.einsum('thc,thc->ht', grad_float, attended.astype(jnp.float32))
        grad_chances = jnp.einsum('thc,lhc->htl', grad_float, value_all)
        grad_scores = (chances * (grad_chances - row_delta[..., None]) * score_scale).astype(jnp.bfloat16)
        grad_scores = lax.optimization_barrier(grad_scores).astype(jnp.float32)
        grad_query = jnp.einsum('htl,lhc->thc', grad_scores, key_all).astype(jnp.bfloat16)
        grad_keys = jnp.einsum('htl,thc->lhc', grad_scores, query_float)
        grad_values = jnp.einsum('htl,thc->lhc', rounded, grad_float)
        carried = (far_grad_keys + grad_keys[near_span:], far_grad_values + grad_values[near_span:])
        return (carried, (attended.reshape(TILE, features), grad_query.reshape(TILE, features), grad_keys[:near_span].reshape(3, TILE, features), grad_values[:near_span].reshape(3, TILE, features)))
    empty_sum = jnp.zeros((N_BLOCKS, HEADS, head_size), dtype=jnp.float32)
    far_sums, block_outs = lax.scan(one_block, (empty_sum, empty_sum), (query_all, grad_all, pattern))
    far_grad_keys, far_grad_values = far_sums
    attended, grad_query, near_grad_keys, near_grad_values = block_outs
    layer_out = jnp.dot(attended.reshape(TOKENS, features), out_weight, preferred_element_type=jnp.float32).astype(jnp.bfloat16)
    flat_ids = pattern.reshape(-1).astype(jnp.int32)
    near_key_sum = jax.ops.segment_sum(near_grad_keys.reshape(N_BLOCKS * 3, TILE * features), flat_ids, num_segments=N_BLOCKS)
    near_value_sum = jax.ops.segment_sum(near_grad_values.reshape(N_BLOCKS * 3, TILE * features), flat_ids, num_segments=N_BLOCKS)
    spread_keys = live_float[:, :, None] * (far_grad_keys.reshape(N_BLOCKS, features) / root_counts[:, None])[:, None, :]
    spread_values = live_float[:, :, None] * (far_grad_values.reshape(N_BLOCKS, features) / root_counts[:, None])[:, None, :]
    grad_keys = (near_key_sum.reshape(N_BLOCKS, TILE, features) + spread_keys).astype(jnp.bfloat16).reshape(TOKENS, features)
    grad_values = (near_value_sum.reshape(N_BLOCKS, TILE, features) + spread_values).astype(jnp.bfloat16).reshape(TOKENS, features)
    return (layer_out, grad_query.reshape(TOKENS, features), grad_keys, grad_values)
```

```python
import functools

import jax
import jax.numpy as jnp
from jax import lax
from jax.experimental import pallas as pl
from jax.experimental.pallas import tpu as pltpu
from jax.sharding import PartitionSpec as P

HEADS = 16
TILE = 128
PAIR = 128
GROUP = 256
AHEAD = 2
F32 = jnp.float32
BF16 = jnp.bfloat16


def nn(a, b):
    return lax.dot_general(a, b, (((1,), (0,)), ((), ())), preferred_element_type=F32)


def nt(a, b):
    return lax.dot_general(a, b, (((1,), (1,)), ((), ())), preferred_element_type=F32)


def tn(a, b):
    return lax.dot_general(a, b, (((0,), (0,)), ((), ())), preferred_element_type=F32)


def kernel(
    count,
    pattern, valid, queries, keys, values, grad_out, weight,
    layer_out, grad_queries, grad_keys, grad_values,
    halo, back_out, back_in, own, attended, grad_att,
    gathered, far_kv, far_sum, far_out, far_in,
    halo_send, halo_recv, back_send, back_recv,
    sum_send, sum_recv, far_send, far_recv,
):
    me = lax.axis_index("lon")
    east = lax.rem(me + 1, count)
    west = lax.rem(me + count - 1, count)
    rows, features = queries.shape
    pairs = features // PAIR
    groups = features // GROUP
    n_blocks = 2 * count
    kv_refs = (keys, values)
    sides = (west, east)

    def peer(step):
        return lax.rem(me + step, count)

    def source(step):
        return lax.rem(me + count - step, count)

    barrier = pltpu.get_barrier_semaphore()

    def greet(step, carry):
        pl.semaphore_signal(
            barrier, inc=1, device_id={"lon": peer(step)}, device_id_type=pl.DeviceIdType.MESH
        )
        return carry

    lax.fori_loop(1, count, greet, 0)
    pl.semaphore_wait(barrier, count - 1)

    def columns(pair):
        return pl.ds(pl.multiple_of(pair * PAIR, PAIR), PAIR)

    def halo_copy(side, kind, pair):
        return pltpu.make_async_remote_copy(
            src_ref=kv_refs[kind].at[:, columns(pair)],
            dst_ref=halo.at[1 - side, kind, :, columns(pair)],
            send_sem=halo_send.at[side, kind, pair],
            recv_sem=halo_recv.at[1 - side, kind, pair],
            device_id={"lon": sides[side]},
            device_id_type=pl.DeviceIdType.MESH,
        )

    def halo_arrival(slot, kind, pair):
        return pltpu.make_async_remote_copy(
            src_ref=kv_refs[kind].at[:, columns(pair)],
            dst_ref=halo.at[slot, kind, :, columns(pair)],
            send_sem=halo_send.at[slot, kind, pair],
            recv_sem=halo_recv.at[slot, kind, pair],
            device_id={"lon": sides[slot]},
            device_id_type=pl.DeviceIdType.MESH,
        )

    def back_copy(side, kind, pair):
        return pltpu.make_async_remote_copy(
            src_ref=back_out.at[side, kind, :, columns(pair)],
            dst_ref=back_in.at[1 - side, kind, :, columns(pair)],
            send_sem=back_send.at[side, kind, pair],
            recv_sem=back_recv.at[1 - side, kind, pair],
            device_id={"lon": sides[side]},
            device_id_type=pl.DeviceIdType.MESH,
        )

    def back_arrival(slot, kind, pair):
        return pltpu.make_async_remote_copy(
            src_ref=back_out.at[slot, kind, :, columns(pair)],
            dst_ref=back_in.at[slot, kind, :, columns(pair)],
            send_sem=back_send.at[slot, kind, pair],
            recv_sem=back_recv.at[slot, kind, pair],
            device_id={"lon": sides[slot]},
            device_id_type=pl.DeviceIdType.MESH,
        )

    def summary_copy(step, slot):
        return pltpu.make_async_remote_copy(
            src_ref=gathered.at[slot],
            dst_ref=gathered.at[slot],
            send_sem=sum_send.at[step],
            recv_sem=sum_recv.at[step],
            device_id={"lon": peer(step)},
            device_id_type=pl.DeviceIdType.MESH,
        )

    def far_copy(step, taken, slot):
        return pltpu.make_async_remote_copy(
            src_ref=far_out.at[taken],
            dst_ref=far_in.at[slot],
            send_sem=far_send.at[step],
            recv_sem=far_recv.at[step],
            device_id={"lon": peer(step)},
            device_id_type=pl.DeviceIdType.MESH,
        )

    def send_halo(pair):
        for kind in range(2):
            for side in range(2):
                halo_copy(side, kind, pair).start()

    send_halo(0)

    own_count = [valid[2 * me + b] for b in range(2)]
    root_row = lax.broadcasted_iota(jnp.int32, (16, GROUP), 0)
    root = jnp.sqrt(
        jnp.where(root_row % 2 == 0, own_count[0], own_count[1]).astype(F32)
    )
    pool_row = lax.broadcasted_iota(jnp.int32, (16, rows), 0)
    pool_col = lax.broadcasted_iota(jnp.int32, (16, rows), 1)
    pool_live = pool_col < jnp.where(pool_col < TILE, own_count[0], own_count[1] + TILE)
    pool_block = jnp.where(pool_col < TILE, 0, 1)
    pooled = jnp.zeros((16, GROUP), F32)
    for c in range(groups):
        for kind in range(2):
            chosen = (pool_row == 4 * c + 2 * kind + pool_block) & pool_live
            pooled += nn(
                chosen.astype(F32).astype(BF16), kv_refs[kind][:, c * GROUP : (c + 1) * GROUP]
            )
    gathered[me] = (pooled / root).astype(BF16)

    def send_summary(step, carry):
        summary_copy(step, me).start()
        return carry

    lax.fori_loop(1, count, send_summary, 0)
    for pair in range(1, AHEAD):
        send_halo(pair)

    for c in range(groups):
        part = slice(c * GROUP, (c + 1) * GROUP)
        grad_att[:, part] = nt(grad_out[...], weight[part, :]).astype(BF16)

    def take_summary(step, carry):
        summary_copy(step, source(step)).wait_recv()
        return carry

    lax.fori_loop(1, count, take_summary, 0)
    pieces = gathered[...].reshape(count * 16, GROUP)
    sel_row = lax.broadcasted_iota(jnp.int32, (n_blocks, count * 16), 0)
    sel_col = lax.broadcasted_iota(jnp.int32, (n_blocks, count * 16), 1)
    sel_place = (sel_row // 2) * 16 + sel_row % 2
    for c in range(groups):
        for kind in range(2):
            chosen = (sel_col == sel_place + (4 * c + 2 * kind)).astype(F32).astype(BF16)
            far_kv[kind, :, c * GROUP : (c + 1) * GROUP] = nn(chosen, pieces).astype(BF16)

    lane = lax.broadcasted_iota(jnp.int32, (1, PAIR), 1)
    first = (lane < PAIR // 2).astype(F32).astype(BF16)
    second = (lane >= PAIR // 2).astype(F32).astype(BF16)
    half = TILE // 2
    key_row = lax.broadcasted_iota(jnp.int32, (half, 2 * TILE), 0) + half
    block_info = []
    for b in range(2):
        west_block = pattern[2 * me + b, 0]
        east_block = pattern[2 * me + b, 2]
        picks = [(lax.rem(blk, 2) == 0) for blk in (west_block, east_block)]
        counts = (valid[west_block], own_count[b], valid[east_block])
        block_info.append((picks, counts))

    def heads_of(tensor):
        return jnp.concatenate((tensor * first, tensor * second), axis=0)

    def unfold(tensor):
        return jnp.concatenate(
            (tensor[: PAIR // 2, :TILE], tensor[PAIR // 2 :, TILE:]), axis=0
        ).T

    def step_pair(pair, carry):
        cols = columns(pair)

        @pl.when(pair + AHEAD < pairs)
        def _():
            send_halo(pair + AHEAD)

        for kind in range(2):
            for slot in range(2):
                halo_arrival(slot, kind, pair).wait_recv()

        edges = []
        far_total = [None, None]
        for b in range(2):
            picks, counts = block_info[b]
            band = pl.ds(b * TILE, TILE)
            sets = []
            for kind in range(2):
                near = []
                for slot in range(2):
                    near.append(
                        lax.select(
                            picks[slot],
                            halo[slot, kind, pl.ds(0, TILE), cols],
                            halo[slot, kind, pl.ds(TILE, TILE), cols],
                        )
                    )
                sets.append(
                    jnp.concatenate(
                        (near[0], kv_refs[kind][band, cols], near[1], far_kv[kind, :, cols]),
                        axis=0,
                    )
                )
            all_keys, all_values = sets
            query = heads_of(queries[band, cols] * jnp.asarray(0.125, BF16))
            grads = heads_of(grad_att[band, cols])
            scores = nt(all_keys, query)
            parts = []
            for slot in range(3):
                base = slot * TILE
                parts.append(scores[base : base + half])
                parts.append(
                    jnp.where(
                        key_row < counts[slot], scores[base + half : base + TILE], -jnp.inf
                    )
                )
            parts.append(scores[3 * TILE :])
            scores = jnp.concatenate(parts, axis=0)
            top = jnp.max(scores, axis=0, keepdims=True)
            weights = jnp.exp(scores - top)
            total = jnp.sum(weights, axis=0, keepdims=True)
            grad_chances = nt(all_values, grads)
            chances = weights * (1.0 / total)
            rounded = chances.astype(BF16)
            delta = jnp.sum(chances * grad_chances, axis=0, keepdims=True)
            grad_scores = (chances * (grad_chances - delta)).astype(BF16)
            attended[band, cols] = unfold(tn(all_values, rounded)).astype(BF16)
            grad_queries[band, cols] = (unfold(tn(all_keys, grad_scores)) * 0.125).astype(BF16)
            results = (nn(grad_scores, query), nn(rounded, grads))
            sides_of = []
            for kind in range(2):
                full = results[kind]
                own[kind, band, cols] = full[TILE : 2 * TILE]
                far = full[3 * TILE :]
                far_total[kind] = far if b == 0 else far_total[kind] + far
                sides_of.append((full[:TILE], full[2 * TILE : 3 * TILE]))
            edges.append(sides_of)

        for kind in range(2):
            far_sum[kind, :, cols] = far_total[kind].astype(BF16)
            for side in range(2):
                low = [jnp.where(block_info[b][0][side], 1.0, 0.0).astype(F32) for b in range(2)]
                one, two = edges[0][kind][side], edges[1][kind][side]
                back_out[side, kind, pl.ds(0, TILE), cols] = (
                    one * low[0] + two * low[1]
                ).astype(BF16)
                back_out[side, kind, pl.ds(TILE, TILE), cols] = (
                    one * (1.0 - low[0]) + two * (1.0 - low[1])
                ).astype(BF16)
        for kind in range(2):
            for side in range(2):
                back_copy(side, kind, pair).start()
        return carry

    lax.fori_loop(0, pairs, step_pair, 0)

    put_row = lax.broadcasted_iota(jnp.int32, (count * 16, n_blocks), 0)
    put_col = lax.broadcasted_iota(jnp.int32, (count * 16, n_blocks), 1)
    put_place = (put_col // 2) * 16 + put_col % 2
    packed = jnp.zeros((count * 16, GROUP), F32)
    for c in range(groups):
        for kind in range(2):
            chosen = (put_row == put_place + (4 * c + 2 * kind)).astype(F32).astype(BF16)
            packed += nn(chosen, far_sum[kind, :, c * GROUP : (c + 1) * GROUP])
    far_out[...] = packed.astype(BF16).reshape(count, 16, GROUP)
    far_in[me] = far_out[me]

    def send_far(step, carry):
        far_copy(step, peer(step), me).start()
        return carry

    lax.fori_loop(1, count, send_far, 0)

    for c in range(groups):
        part = slice(c * GROUP, (c + 1) * GROUP)
        layer_out[:, part] = nn(attended[...], weight[:, part]).astype(BF16)

    def take_far(step, carry):
        far_copy(step, peer(step), source(step)).wait_recv()
        return carry

    lax.fori_loop(1, count, take_far, 0)
    spread = jnp.sum(far_in[...].astype(F32), axis=0) / root
    live_row = lax.broadcasted_iota(jnp.int32, (TILE, GROUP), 0)
    outs = (grad_keys, grad_values)
    for c in range(groups):
        part = slice(c * GROUP, (c + 1) * GROUP)
        for pair in range(c * GROUP // PAIR, (c + 1) * GROUP // PAIR):
            for kind in range(2):
                for slot in range(2):
                    back_arrival(slot, kind, pair).wait_recv()
        for kind in range(2):
            for b in range(2):
                band = slice(b * TILE, (b + 1) * TILE)
                line = 4 * c + 2 * kind + b
                far = jnp.where(live_row < own_count[b], spread[line : line + 1, :], 0.0)
                outs[kind][band, part] = (
                    own[kind, band, part]
                    + back_in[0, kind, band, part].astype(F32)
                    + back_in[1, kind, band, part].astype(F32)
                    + far
                ).astype(BF16)

    def drain_pair(pair, carry):
        for kind in range(2):
            for side in range(2):
                halo_copy(side, kind, pair).wait_send()
                back_copy(side, kind, pair).wait_send()
        return carry

    lax.fori_loop(0, pairs, drain_pair, 0)

    def drain_peer(step, carry):
        summary_copy(step, me).wait_send()
        far_copy(step, peer(step), me).wait_send()
        return carry

    lax.fori_loop(1, count, drain_peer, 0)


def per_device(queries, key_tokens, value_tokens, grad_out, out_weight, pattern, valid_rows):
    count = lax.axis_size("lon")
    rows, features = queries.shape
    n_blocks = 2 * count
    pairs = features // PAIR
    shape = jax.ShapeDtypeStruct((rows, features), BF16)
    vmem = pl.BlockSpec(memory_space=pltpu.VMEM)
    smem = pl.BlockSpec(memory_space=pltpu.SMEM)
    dma = pltpu.SemaphoreType.DMA
    return pl.pallas_call(
        functools.partial(kernel, count),
        out_shape=(shape,) * 4,
        in_specs=[smem, smem] + [vmem] * 5,
        out_specs=(vmem,) * 4,
        scratch_shapes=[
            pltpu.VMEM((2, 2, rows, features), BF16),
            pltpu.VMEM((2, 2, rows, features), BF16),
            pltpu.VMEM((2, 2, rows, features), BF16),
            pltpu.VMEM((2, rows, features), F32),
            pltpu.VMEM((rows, features), BF16),
            pltpu.VMEM((rows, features), BF16),
            pltpu.VMEM((count, 16, GROUP), BF16),
            pltpu.VMEM((2, n_blocks, features), BF16),
            pltpu.VMEM((2, n_blocks, features), BF16),
            pltpu.VMEM((count, 16, GROUP), BF16),
            pltpu.VMEM((count, 16, GROUP), BF16),
            dma((2, 2, pairs)),
            dma((2, 2, pairs)),
            dma((2, 2, pairs)),
            dma((2, 2, pairs)),
            dma((count,)),
            dma((count,)),
            dma((count,)),
            dma((count,)),
        ],
        compiler_params=pltpu.CompilerParams(
            collective_id=0, has_side_effects=True, vmem_limit_bytes=48 * 2**20
        ),
        cost_estimate=pl.CostEstimate(
            flops=2_600_000_000, bytes_accessed=6_500_000, transcendentals=1_800_000
        ),
    )(pattern, valid_rows, queries, key_tokens, value_tokens, grad_out, out_weight)


def solution(mesh):
    split = P(("groups", "lon"), None)
    return jax.shard_map(
        per_device,
        mesh=mesh,
        in_specs=(split, split, split, split, P(), P(), P()),
        out_specs=(split,) * 4,
        check_vma=False,
    )
```

```python
import functools

import jax
import jax.numpy as jnp
from jax import lax
from jax.experimental import pallas as pl
from jax.experimental.pallas import tpu as pltpu
from jax.sharding import PartitionSpec as P

HEADS = 16
TILE = 128
PAIR = 128
GROUP = 256
BEFORE = 1
AHEAD = 4
F32 = jnp.float32
BF16 = jnp.bfloat16


def nn(a, b):
    return lax.dot_general(a, b, (((1,), (0,)), ((), ())), preferred_element_type=F32)


def nt(a, b):
    return lax.dot_general(a, b, (((1,), (1,)), ((), ())), preferred_element_type=F32)


def tn(a, b):
    return lax.dot_general(a, b, (((0,), (0,)), ((), ())), preferred_element_type=F32)


def kernel(
    count,
    pattern, valid, queries_hbm, keys_hbm, values_hbm, grad_out_hbm, weight_hbm,
    layer_out_hbm, grad_queries_hbm, grad_keys_hbm, grad_values_hbm,
    queries, keys, values, grad_out, weight,
    layer_out, grad_queries, grad_keys, grad_values, load_sem, store_sem,
    halo, back_out, back_in, own, attended, grad_att,
    gathered, far_kv, far_sum, far_out, far_in,
    halo_send, halo_recv, back_send, back_recv,
    sum_send, sum_recv, far_send, far_recv,
):
    me = lax.axis_index("lon")
    east = lax.rem(me + 1, count)
    west = lax.rem(me + count - 1, count)
    rows, features = queries.shape
    pairs = features // PAIR
    groups = features // GROUP
    n_blocks = 2 * count
    kv_refs = (keys, values)
    sides = (west, east)

    def peer(step):
        return lax.rem(me + step, count)

    def source(step):
        return lax.rem(me + count - step, count)

    barrier = pltpu.get_barrier_semaphore()

    def greet(step, carry):
        pl.semaphore_signal(
            barrier, inc=1, device_id={"lon": peer(step)}, device_id_type=pl.DeviceIdType.MESH
        )
        return carry

    lax.fori_loop(1, count, greet, 0)
    loads = [
        pltpu.make_async_copy(far, near, load_sem.at[i])
        for i, (far, near) in enumerate(
            (
                (keys_hbm, keys),
                (values_hbm, values),
                (grad_out_hbm, grad_out),
                (weight_hbm, weight),
                (queries_hbm, queries),
            )
        )
    ]
    for load in loads:
        load.start()
    loads[0].wait()
    loads[1].wait()

    def columns(pair):
        return pl.ds(pl.multiple_of(pair * PAIR, PAIR), PAIR)

    def halo_copy(side, kind, pair):
        return pltpu.make_async_remote_copy(
            src_ref=kv_refs[kind].at[:, columns(pair)],
            dst_ref=halo.at[1 - side, kind, :, columns(pair)],
            send_sem=halo_send.at[side, kind, pair],
            recv_sem=halo_recv.at[1 - side, kind, pair],
            device_id={"lon": sides[side]},
            device_id_type=pl.DeviceIdType.MESH,
        )

    def halo_arrival(slot, kind, pair):
        return pltpu.make_async_remote_copy(
            src_ref=kv_refs[kind].at[:, columns(pair)],
            dst_ref=halo.at[slot, kind, :, columns(pair)],
            send_sem=halo_send.at[slot, kind, pair],
            recv_sem=halo_recv.at[slot, kind, pair],
            device_id={"lon": sides[slot]},
            device_id_type=pl.DeviceIdType.MESH,
        )

    def back_copy(side, kind, pair):
        return pltpu.make_async_remote_copy(
            src_ref=back_out.at[side, kind, :, columns(pair)],
            dst_ref=back_in.at[1 - side, kind, :, columns(pair)],
            send_sem=back_send.at[side, kind, pair],
            recv_sem=back_recv.at[1 - side, kind, pair],
            device_id={"lon": sides[side]},
            device_id_type=pl.DeviceIdType.MESH,
        )

    def back_arrival(slot, kind, pair):
        return pltpu.make_async_remote_copy(
            src_ref=back_out.at[slot, kind, :, columns(pair)],
            dst_ref=back_in.at[slot, kind, :, columns(pair)],
            send_sem=back_send.at[slot, kind, pair],
            recv_sem=back_recv.at[slot, kind, pair],
            device_id={"lon": sides[slot]},
            device_id_type=pl.DeviceIdType.MESH,
        )

    def summary_copy(step, slot):
        return pltpu.make_async_remote_copy(
            src_ref=gathered.at[slot],
            dst_ref=gathered.at[slot],
            send_sem=sum_send.at[step],
            recv_sem=sum_recv.at[step],
            device_id={"lon": peer(step)},
            device_id_type=pl.DeviceIdType.MESH,
        )

    def far_copy(step, taken, slot):
        return pltpu.make_async_remote_copy(
            src_ref=far_out.at[taken],
            dst_ref=far_in.at[slot],
            send_sem=far_send.at[step],
            recv_sem=far_recv.at[step],
            device_id={"lon": peer(step)},
            device_id_type=pl.DeviceIdType.MESH,
        )

    def send_halo(pair):
        for kind in range(2):
            for side in range(2):
                halo_copy(side, kind, pair).start()

    own_count = [valid[2 * me + b] for b in range(2)]
    root_row = lax.broadcasted_iota(jnp.int32, (16, GROUP), 0)
    root = jnp.sqrt(
        jnp.where(root_row % 2 == 0, own_count[0], own_count[1]).astype(F32)
    )
    pool_row = lax.broadcasted_iota(jnp.int32, (16, rows), 0)
    pool_col = lax.broadcasted_iota(jnp.int32, (16, rows), 1)
    pool_live = pool_col < jnp.where(pool_col < TILE, own_count[0], own_count[1] + TILE)
    pool_block = jnp.where(pool_col < TILE, 0, 1)
    pooled = jnp.zeros((16, GROUP), F32)
    for c in range(groups):
        for kind in range(2):
            chosen = (pool_row == 4 * c + 2 * kind + pool_block) & pool_live
            pooled += nn(
                chosen.astype(F32).astype(BF16), kv_refs[kind][:, c * GROUP : (c + 1) * GROUP]
            )
    gathered[me] = (pooled / root).astype(BF16)

    def send_summary(step, carry):
        summary_copy(step, me).start()
        return carry

    pl.semaphore_wait(barrier, count - 1)
    lax.fori_loop(1, count, send_summary, 0)
    for pair in range(BEFORE):
        send_halo(pair)

    for load in loads[2:]:
        load.wait()
    part = slice(0, GROUP)
    grad_att[:, part] = nt(grad_out[...], weight[part, :]).astype(BF16)

    def take_summary(step, carry):
        summary_copy(step, source(step)).wait_recv()
        return carry

    lax.fori_loop(1, count, take_summary, 0)
    for pair in range(BEFORE, AHEAD):
        send_halo(pair)
    for c in range(1, groups):
        part = slice(c * GROUP, (c + 1) * GROUP)
        grad_att[:, part] = nt(grad_out[...], weight[part, :]).astype(BF16)
    pieces = gathered[...].reshape(count * 16, GROUP)
    sel_row = lax.broadcasted_iota(jnp.int32, (n_blocks, count * 16), 0)
    sel_col = lax.broadcasted_iota(jnp.int32, (n_blocks, count * 16), 1)
    sel_place = (sel_row // 2) * 16 + sel_row % 2
    for c in range(groups):
        for kind in range(2):
            chosen = (sel_col == sel_place + (4 * c + 2 * kind)).astype(F32).astype(BF16)
            far_kv[kind, :, c * GROUP : (c + 1) * GROUP] = nn(chosen, pieces).astype(BF16)

    lane = lax.broadcasted_iota(jnp.int32, (1, PAIR), 1)
    first = (lane < PAIR // 2).astype(F32).astype(BF16)
    second = (lane >= PAIR // 2).astype(F32).astype(BF16)
    half = TILE // 2
    key_row = lax.broadcasted_iota(jnp.int32, (half, 2 * TILE), 0) + half
    block_info = []
    for b in range(2):
        west_block = pattern[0, 2 * me + b]
        east_block = pattern[2, 2 * me + b]
        picks = [(lax.rem(blk, 2) == 0) for blk in (west_block, east_block)]
        counts = (valid[west_block], own_count[b], valid[east_block])
        block_info.append((picks, counts))

    def heads_of(tensor):
        return jnp.concatenate((tensor * first, tensor * second), axis=0)

    def unfold(tensor):
        return jnp.concatenate(
            (tensor[: PAIR // 2, :TILE], tensor[PAIR // 2 :, TILE:]), axis=0
        ).T

    def step_pair(pair, carry):
        cols = columns(pair)

        @pl.when(pair + AHEAD < pairs)
        def _():
            send_halo(pair + AHEAD)

        for kind in range(2):
            for slot in range(2):
                halo_arrival(slot, kind, pair).wait_recv()

        edges = []
        far_total = [None, None]
        for b in range(2):
            picks, counts = block_info[b]
            band = pl.ds(b * TILE, TILE)
            sets = []
            for kind in range(2):
                near = []
                for slot in range(2):
                    near.append(
                        lax.select(
                            picks[slot],
                            halo[slot, kind, pl.ds(0, TILE), cols],
                            halo[slot, kind, pl.ds(TILE, TILE), cols],
                        )
                    )
                sets.append(
                    jnp.concatenate(
                        (near[0], kv_refs[kind][band, cols], near[1], far_kv[kind, :, cols]),
                        axis=0,
                    )
                )
            all_keys, all_values = sets
            query = heads_of(queries[band, cols] * jnp.asarray(0.125, BF16))
            grads = heads_of(grad_att[band, cols])
            scores = nt(all_keys, query)
            parts = []
            for slot in range(3):
                base = slot * TILE
                parts.append(scores[base : base + half])
                parts.append(
                    jnp.where(
                        key_row < counts[slot], scores[base + half : base + TILE], -jnp.inf
                    )
                )
            parts.append(scores[3 * TILE :])
            scores = jnp.concatenate(parts, axis=0)
            top = jnp.max(scores, axis=0, keepdims=True)
            weights = jnp.exp(scores - top)
            total = jnp.sum(weights, axis=0, keepdims=True)
            grad_chances = nt(all_values, grads)
            chances = weights * (1.0 / total)
            rounded = chances.astype(BF16)
            delta = jnp.sum(chances * grad_chances, axis=0, keepdims=True)
            grad_scores = (chances * (grad_chances - delta)).astype(BF16)
            attended[band, cols] = unfold(tn(all_values, rounded)).astype(BF16)
            grad_queries[band, cols] = (unfold(tn(all_keys, grad_scores)) * 0.125).astype(BF16)
            results = (nn(grad_scores, query), nn(rounded, grads))
            sides_of = []
            for kind in range(2):
                full = results[kind]
                own[kind, band, cols] = full[TILE : 2 * TILE]
                far = full[3 * TILE :]
                far_total[kind] = far if b == 0 else far_total[kind] + far
                sides_of.append((full[:TILE], full[2 * TILE : 3 * TILE]))
            edges.append(sides_of)

        for kind in range(2):
            far_sum[kind, :, cols] = far_total[kind].astype(BF16)
            for side in range(2):
                low = [jnp.where(block_info[b][0][side], 1.0, 0.0).astype(F32) for b in range(2)]
                one, two = edges[0][kind][side], edges[1][kind][side]
                back_out[side, kind, pl.ds(0, TILE), cols] = (
                    one * low[0] + two * low[1]
                ).astype(BF16)
                back_out[side, kind, pl.ds(TILE, TILE), cols] = (
                    one * (1.0 - low[0]) + two * (1.0 - low[1])
                ).astype(BF16)
        for kind in range(2):
            for side in range(2):
                back_copy(side, kind, pair).start()
        return carry

    lax.fori_loop(0, pairs, step_pair, 0)

    put_row = lax.broadcasted_iota(jnp.int32, (count * 16, n_blocks), 0)
    put_col = lax.broadcasted_iota(jnp.int32, (count * 16, n_blocks), 1)
    put_place = (put_col // 2) * 16 + put_col % 2
    packed = jnp.zeros((count * 16, GROUP), F32)
    for c in range(groups):
        for kind in range(2):
            chosen = (put_row == put_place + (4 * c + 2 * kind)).astype(F32).astype(BF16)
            packed += nn(chosen, far_sum[kind, :, c * GROUP : (c + 1) * GROUP])
    far_out[...] = packed.astype(BF16).reshape(count, 16, GROUP)
    far_in[me] = far_out[me]

    def send_far(step, carry):
        far_copy(step, peer(step), me).start()
        return carry

    lax.fori_loop(1, count, send_far, 0)

    for c in range(groups):
        part = slice(c * GROUP, (c + 1) * GROUP)
        layer_out[:, part] = nn(attended[...], weight[:, part]).astype(BF16)
    stores = [
        pltpu.make_async_copy(layer_out, layer_out_hbm, store_sem.at[0]),
        pltpu.make_async_copy(grad_queries, grad_queries_hbm, store_sem.at[1]),
    ]
    for store in stores:
        store.start()

    def take_far(step, carry):
        far_copy(step, peer(step), source(step)).wait_recv()
        return carry

    lax.fori_loop(1, count, take_far, 0)
    spread = jnp.sum(far_in[...].astype(F32), axis=0) / root
    live_row = lax.broadcasted_iota(jnp.int32, (TILE, GROUP), 0)
    outs = (grad_keys, grad_values)
    outs_hbm = (grad_keys_hbm, grad_values_hbm)
    for c in range(groups):
        part = slice(c * GROUP, (c + 1) * GROUP)
        for pair in range(c * GROUP // PAIR, (c + 1) * GROUP // PAIR):
            for kind in range(2):
                for slot in range(2):
                    back_arrival(slot, kind, pair).wait_recv()
        for kind in range(2):
            for b in range(2):
                band = slice(b * TILE, (b + 1) * TILE)
                line = 4 * c + 2 * kind + b
                far = jnp.where(live_row < own_count[b], spread[line : line + 1, :], 0.0)
                outs[kind][band, part] = (
                    own[kind, band, part]
                    + back_in[0, kind, band, part].astype(F32)
                    + back_in[1, kind, band, part].astype(F32)
                    + far
                ).astype(BF16)
            store = pltpu.make_async_copy(
                outs[kind].at[:, part], outs_hbm[kind].at[:, part], store_sem.at[2 + 2 * c + kind]
            )
            store.start()
            stores.append(store)

    def drain_pair(pair, carry):
        for kind in range(2):
            for side in range(2):
                halo_copy(side, kind, pair).wait_send()
                back_copy(side, kind, pair).wait_send()
        return carry

    lax.fori_loop(0, pairs, drain_pair, 0)

    def drain_peer(step, carry):
        summary_copy(step, me).wait_send()
        far_copy(step, peer(step), me).wait_send()
        return carry

    lax.fori_loop(1, count, drain_peer, 0)
    for store in stores:
        store.wait()


def hand_over(*refs):
    sources, targets, sems = refs[:4], refs[4:8], refs[8]
    copies = [
        pltpu.make_async_copy(sources[i], targets[i], sems.at[i]) for i in range(4)
    ]
    for copy in copies:
        copy.start()
    for copy in copies:
        copy.wait()


def per_device(queries, key_tokens, value_tokens, grad_out, out_weight, pattern, valid_rows):
    count = lax.axis_size("lon")
    rows, features = queries.shape
    n_blocks = 2 * count
    pairs = features // PAIR
    shape = jax.ShapeDtypeStruct((rows, features), BF16)
    hbm = pl.BlockSpec(memory_space=pltpu.HBM)
    smem = pl.BlockSpec(memory_space=pltpu.SMEM)
    dma = pltpu.SemaphoreType.DMA
    outs = pl.pallas_call(
        functools.partial(kernel, count),
        out_shape=(shape,) * 4,
        in_specs=[smem, smem] + [hbm] * 5,
        out_specs=(hbm,) * 4,
        scratch_shapes=[
            pltpu.VMEM((rows, features), BF16),
            pltpu.VMEM((rows, features), BF16),
            pltpu.VMEM((rows, features), BF16),
            pltpu.VMEM((rows, features), BF16),
            pltpu.VMEM((features, features), BF16),
            pltpu.VMEM((rows, features), BF16),
            pltpu.VMEM((rows, features), BF16),
            pltpu.VMEM((rows, features), BF16),
            pltpu.VMEM((rows, features), BF16),
            dma((5,)),
            dma((2 + 2 * (features // GROUP),)),
            pltpu.VMEM((2, 2, rows, features), BF16),
            pltpu.VMEM((2, 2, rows, features), BF16),
            pltpu.VMEM((2, 2, rows, features), BF16),
            pltpu.VMEM((2, rows, features), F32),
            pltpu.VMEM((rows, features), BF16),
            pltpu.VMEM((rows, features), BF16),
            pltpu.VMEM((count, 16, GROUP), BF16),
            pltpu.VMEM((2, n_blocks, features), BF16),
            pltpu.VMEM((2, n_blocks, features), BF16),
            pltpu.VMEM((count, 16, GROUP), BF16),
            pltpu.VMEM((count, 16, GROUP), BF16),
            dma((2, 2, pairs)),
            dma((2, 2, pairs)),
            dma((2, 2, pairs)),
            dma((2, 2, pairs)),
            dma((count,)),
            dma((count,)),
            dma((count,)),
            dma((count,)),
        ],
        compiler_params=pltpu.CompilerParams(
            collective_id=0, has_side_effects=True, vmem_limit_bytes=63 * 2**20
        ),
        cost_estimate=pl.CostEstimate(
            flops=2_600_000_000, bytes_accessed=6_500_000, transcendentals=1_800_000
        ),
    )(pattern.T, valid_rows, queries, key_tokens, value_tokens, grad_out, out_weight)
    return pl.pallas_call(
        hand_over,
        out_shape=(shape,) * 4,
        in_specs=[hbm] * 4,
        out_specs=(hbm,) * 4,
        scratch_shapes=[dma((4,))],
    )(*outs)


def solution(mesh):
    split = P(("groups", "lon"), None)
    return jax.shard_map(
        per_device,
        mesh=mesh,
        in_specs=(split, split, split, split, P(), P(), P()),
        out_specs=(split,) * 4,
        check_vma=False,
    )
```

```python
import functools

import jax
import jax.numpy as jnp
from jax import lax
from jax.experimental import pallas as pl
from jax.experimental.pallas import tpu as pltpu
from jax.sharding import PartitionSpec as P

HEADS = 16
TILE = 128
PAIR = 128
GROUP = 256
BEFORE = 2
AHEAD = 4
F32 = jnp.float32
BF16 = jnp.bfloat16


def nn(a, b):
    return lax.dot_general(a, b, (((1,), (0,)), ((), ())), preferred_element_type=F32)


def nt(a, b):
    return lax.dot_general(a, b, (((1,), (1,)), ((), ())), preferred_element_type=F32)


def tn(a, b):
    return lax.dot_general(a, b, (((0,), (0,)), ((), ())), preferred_element_type=F32)


def kernel(
    count,
    pattern, valid, queries_hbm, keys_hbm, values_hbm, grad_out_hbm, weight_hbm,
    layer_out_hbm, grad_queries_hbm, grad_keys_hbm, grad_values_hbm,
    queries, keys, values, grad_out, weight,
    layer_out, grad_queries, grad_keys, grad_values, load_sem, store_sem,
    halo, back_out, back_in, own, attended, grad_att,
    gathered, far_kv, far_sum, far_out, far_in,
    halo_send, halo_recv, back_send, back_recv,
    sum_send, sum_recv, far_send, far_recv,
):
    me = lax.axis_index("lon")
    east = lax.rem(me + 1, count)
    west = lax.rem(me + count - 1, count)
    rows, features = queries.shape
    pairs = features // PAIR
    groups = features // GROUP
    n_blocks = 2 * count
    kv_refs = (keys, values)
    sides = (west, east)

    def peer(step):
        return lax.rem(me + step, count)

    def source(step):
        return lax.rem(me + count - step, count)

    barrier = pltpu.get_barrier_semaphore()

    def greet(step, carry):
        pl.semaphore_signal(
            barrier, inc=1, device_id={"lon": peer(step)}, device_id_type=pl.DeviceIdType.MESH
        )
        return carry

    lax.fori_loop(1, count, greet, 0)
    loads = [
        pltpu.make_async_copy(far, near, load_sem.at[i])
        for i, (far, near) in enumerate(
            (
                (keys_hbm, keys),
                (values_hbm, values),
                (grad_out_hbm, grad_out),
                (weight_hbm, weight),
                (queries_hbm, queries),
            )
        )
    ]
    for load in loads:
        load.start()
    loads[0].wait()
    loads[1].wait()

    def columns(pair):
        return pl.ds(pl.multiple_of(pair * PAIR, PAIR), PAIR)

    def halo_copy(side, kind, pair):
        return pltpu.make_async_remote_copy(
            src_ref=kv_refs[kind].at[:, columns(pair)],
            dst_ref=halo.at[1 - side, kind, :, columns(pair)],
            send_sem=halo_send.at[side, kind, pair],
            recv_sem=halo_recv.at[1 - side, kind, pair],
            device_id={"lon": sides[side]},
            device_id_type=pl.DeviceIdType.MESH,
        )

    def halo_arrival(slot, kind, pair):
        return pltpu.make_async_remote_copy(
            src_ref=kv_refs[kind].at[:, columns(pair)],
            dst_ref=halo.at[slot, kind, :, columns(pair)],
            send_sem=halo_send.at[slot, kind, pair],
            recv_sem=halo_recv.at[slot, kind, pair],
            device_id={"lon": sides[slot]},
            device_id_type=pl.DeviceIdType.MESH,
        )

    def back_copy(side, kind, pair):
        return pltpu.make_async_remote_copy(
            src_ref=back_out.at[side, kind, :, columns(pair)],
            dst_ref=back_in.at[1 - side, kind, :, columns(pair)],
            send_sem=back_send.at[side, kind, pair],
            recv_sem=back_recv.at[1 - side, kind, pair],
            device_id={"lon": sides[side]},
            device_id_type=pl.DeviceIdType.MESH,
        )

    def back_arrival(slot, kind, pair):
        return pltpu.make_async_remote_copy(
            src_ref=back_out.at[slot, kind, :, columns(pair)],
            dst_ref=back_in.at[slot, kind, :, columns(pair)],
            send_sem=back_send.at[slot, kind, pair],
            recv_sem=back_recv.at[slot, kind, pair],
            device_id={"lon": sides[slot]},
            device_id_type=pl.DeviceIdType.MESH,
        )

    def summary_copy(step, slot):
        return pltpu.make_async_remote_copy(
            src_ref=gathered.at[slot],
            dst_ref=gathered.at[slot],
            send_sem=sum_send.at[step],
            recv_sem=sum_recv.at[step],
            device_id={"lon": peer(step)},
            device_id_type=pl.DeviceIdType.MESH,
        )

    def far_copy(step, taken, slot):
        return pltpu.make_async_remote_copy(
            src_ref=far_out.at[taken],
            dst_ref=far_in.at[slot],
            send_sem=far_send.at[step],
            recv_sem=far_recv.at[step],
            device_id={"lon": peer(step)},
            device_id_type=pl.DeviceIdType.MESH,
        )

    def send_halo(pair):
        for kind in range(2):
            for side in range(2):
                halo_copy(side, kind, pair).start()

    own_count = [valid[2 * me + b] for b in range(2)]
    root_row = lax.broadcasted_iota(jnp.int32, (16, GROUP), 0)
    root = jnp.sqrt(
        jnp.where(root_row % 2 == 0, own_count[0], own_count[1]).astype(F32)
    )
    pool_row = lax.broadcasted_iota(jnp.int32, (16, rows), 0)
    pool_col = lax.broadcasted_iota(jnp.int32, (16, rows), 1)
    pool_live = pool_col < jnp.where(pool_col < TILE, own_count[0], own_count[1] + TILE)
    pool_block = jnp.where(pool_col < TILE, 0, 1)
    pooled = jnp.zeros((16, GROUP), F32)
    for c in range(groups):
        for kind in range(2):
            chosen = (pool_row == 4 * c + 2 * kind + pool_block) & pool_live
            pooled += nn(
                chosen.astype(F32).astype(BF16), kv_refs[kind][:, c * GROUP : (c + 1) * GROUP]
            )
    gathered[me] = (pooled / root).astype(BF16)

    def send_summary(step, carry):
        summary_copy(step, me).start()
        return carry

    pl.semaphore_wait(barrier, count - 1)
    lax.fori_loop(1, count, send_summary, 0)
    for pair in range(BEFORE):
        send_halo(pair)

    for load in loads[2:]:
        load.wait()
    part = slice(0, GROUP)
    grad_att[:, part] = nt(grad_out[...], weight[part, :]).astype(BF16)

    def take_summary(step, carry):
        summary_copy(step, source(step)).wait_recv()
        return carry

    lax.fori_loop(1, count, take_summary, 0)
    for pair in range(BEFORE, AHEAD):
        send_halo(pair)
    for c in range(1, groups):
        part = slice(c * GROUP, (c + 1) * GROUP)
        grad_att[:, part] = nt(grad_out[...], weight[part, :]).astype(BF16)
    pieces = gathered[...].reshape(count * 16, GROUP)
    sel_row = lax.broadcasted_iota(jnp.int32, (n_blocks, count * 16), 0)
    sel_col = lax.broadcasted_iota(jnp.int32, (n_blocks, count * 16), 1)
    sel_place = (sel_row // 2) * 16 + sel_row % 2
    for c in range(groups):
        for kind in range(2):
            chosen = (sel_col == sel_place + (4 * c + 2 * kind)).astype(F32).astype(BF16)
            far_kv[kind, :, c * GROUP : (c + 1) * GROUP] = nn(chosen, pieces).astype(BF16)

    lane = lax.broadcasted_iota(jnp.int32, (1, PAIR), 1)
    first = (lane < PAIR // 2).astype(F32).astype(BF16)
    second = (lane >= PAIR // 2).astype(F32).astype(BF16)
    half = TILE // 2
    key_row = lax.broadcasted_iota(jnp.int32, (half, 2 * TILE), 0) + half
    block_info = []
    for b in range(2):
        west_block = pattern[0, 2 * me + b]
        east_block = pattern[2, 2 * me + b]
        picks = [(lax.rem(blk, 2) == 0) for blk in (west_block, east_block)]
        counts = (valid[west_block], own_count[b], valid[east_block])
        block_info.append((picks, counts))

    def heads_of(tensor):
        return jnp.concatenate((tensor * first, tensor * second), axis=0)

    def unfold(tensor):
        return jnp.concatenate(
            (tensor[: PAIR // 2, :TILE], tensor[PAIR // 2 :, TILE:]), axis=0
        ).T

    def step_pair(pair, carry):
        cols = columns(pair)

        @pl.when(pair + AHEAD < pairs)
        def _():
            send_halo(pair + AHEAD)

        for kind in range(2):
            for slot in range(2):
                halo_arrival(slot, kind, pair).wait_recv()

        edges = []
        far_total = [None, None]
        for b in range(2):
            picks, counts = block_info[b]
            band = pl.ds(b * TILE, TILE)
            sets = []
            for kind in range(2):
                near = []
                for slot in range(2):
                    near.append(
                        lax.select(
                            picks[slot],
                            halo[slot, kind, pl.ds(0, TILE), cols],
                            halo[slot, kind, pl.ds(TILE, TILE), cols],
                        )
                    )
                sets.append(
                    jnp.concatenate(
                        (near[0], kv_refs[kind][band, cols], near[1], far_kv[kind, :, cols]),
                        axis=0,
                    )
                )
            all_keys, all_values = sets
            query = heads_of(queries[band, cols] * jnp.asarray(0.125, BF16))
            grads = heads_of(grad_att[band, cols])
            scores = nt(all_keys, query)
            parts = []
            for slot in range(3):
                base = slot * TILE
                parts.append(scores[base : base + half])
                parts.append(
                    jnp.where(
                        key_row < counts[slot], scores[base + half : base + TILE], -jnp.inf
                    )
                )
            parts.append(scores[3 * TILE :])
            scores = jnp.concatenate(parts, axis=0)
            top = jnp.max(scores, axis=0, keepdims=True)
            weights = jnp.exp(scores - top)
            total = jnp.sum(weights, axis=0, keepdims=True)
            grad_chances = nt(all_values, grads)
            chances = weights * (1.0 / total)
            rounded = chances.astype(BF16)
            delta = jnp.sum(chances * grad_chances, axis=0, keepdims=True)
            grad_scores = (chances * (grad_chances - delta)).astype(BF16)
            attended[band, cols] = unfold(tn(all_values, rounded)).astype(BF16)
            grad_queries[band, cols] = (unfold(tn(all_keys, grad_scores)) * 0.125).astype(BF16)
            results = (nn(grad_scores, query), nn(rounded, grads))
            sides_of = []
            for kind in range(2):
                full = results[kind]
                own[kind, band, cols] = full[TILE : 2 * TILE]
                far = full[3 * TILE :]
                far_total[kind] = far if b == 0 else far_total[kind] + far
                sides_of.append((full[:TILE], full[2 * TILE : 3 * TILE]))
            edges.append(sides_of)

        for kind in range(2):
            far_sum[kind, :, cols] = far_total[kind].astype(BF16)
            for side in range(2):
                low = [jnp.where(block_info[b][0][side], 1.0, 0.0).astype(F32) for b in range(2)]
                one, two = edges[0][kind][side], edges[1][kind][side]
                back_out[side, kind, pl.ds(0, TILE), cols] = (
                    one * low[0] + two * low[1]
                ).astype(BF16)
                back_out[side, kind, pl.ds(TILE, TILE), cols] = (
                    one * (1.0 - low[0]) + two * (1.0 - low[1])
                ).astype(BF16)
        for kind in range(2):
            for side in range(2):
                back_copy(side, kind, pair).start()
        return carry

    lax.fori_loop(0, pairs, step_pair, 0)

    put_row = lax.broadcasted_iota(jnp.int32, (count * 16, n_blocks), 0)
    put_col = lax.broadcasted_iota(jnp.int32, (count * 16, n_blocks), 1)
    put_place = (put_col // 2) * 16 + put_col % 2
    packed = jnp.zeros((count * 16, GROUP), F32)
    for c in range(groups):
        for kind in range(2):
            chosen = (put_row == put_place + (4 * c + 2 * kind)).astype(F32).astype(BF16)
            packed += nn(chosen, far_sum[kind, :, c * GROUP : (c + 1) * GROUP])
    far_out[...] = packed.astype(BF16).reshape(count, 16, GROUP)
    far_in[me] = far_out[me]

    def send_far(step, carry):
        far_copy(step, peer(step), me).start()
        return carry

    lax.fori_loop(1, count, send_far, 0)

    for c in range(groups):
        part = slice(c * GROUP, (c + 1) * GROUP)
        layer_out[:, part] = nn(attended[...], weight[:, part]).astype(BF16)
    stores = [
        pltpu.make_async_copy(layer_out, layer_out_hbm, store_sem.at[0]),
        pltpu.make_async_copy(grad_queries, grad_queries_hbm, store_sem.at[1]),
    ]
    for store in stores:
        store.start()

    def take_far(step, carry):
        far_copy(step, peer(step), source(step)).wait_recv()
        return carry

    lax.fori_loop(1, count, take_far, 0)
    spread = jnp.sum(far_in[...].astype(F32), axis=0) / root
    live_row = lax.broadcasted_iota(jnp.int32, (TILE, GROUP), 0)
    outs = (grad_keys, grad_values)
    outs_hbm = (grad_keys_hbm, grad_values_hbm)
    for c in range(groups):
        part = slice(c * GROUP, (c + 1) * GROUP)
        for pair in range(c * GROUP // PAIR, (c + 1) * GROUP // PAIR):
            for kind in range(2):
                for slot in range(2):
                    back_arrival(slot, kind, pair).wait_recv()
        for kind in range(2):
            for b in range(2):
                band = slice(b * TILE, (b + 1) * TILE)
                line = 4 * c + 2 * kind + b
                far = jnp.where(live_row < own_count[b], spread[line : line + 1, :], 0.0)
                outs[kind][band, part] = (
                    own[kind, band, part]
                    + back_in[0, kind, band, part].astype(F32)
                    + back_in[1, kind, band, part].astype(F32)
                    + far
                ).astype(BF16)
            store = pltpu.make_async_copy(
                outs[kind].at[:, part], outs_hbm[kind].at[:, part], store_sem.at[2 + 2 * c + kind]
            )
            store.start()
            stores.append(store)

    def drain_pair(pair, carry):
        for kind in range(2):
            for side in range(2):
                halo_copy(side, kind, pair).wait_send()
                back_copy(side, kind, pair).wait_send()
        return carry

    lax.fori_loop(0, pairs, drain_pair, 0)

    def drain_peer(step, carry):
        summary_copy(step, me).wait_send()
        far_copy(step, peer(step), me).wait_send()
        return carry

    lax.fori_loop(1, count, drain_peer, 0)
    for store in stores:
        store.wait()


def hand_over(*refs):
    sources, targets, buffers, load_sem, store_sem = refs[:4], refs[4:8], refs[8], refs[9], refs[10]
    loads = [pltpu.make_async_copy(sources[i], buffers.at[i], load_sem.at[i]) for i in range(4)]
    stores = [pltpu.make_async_copy(buffers.at[i], targets[i], store_sem.at[i]) for i in range(4)]
    for load in loads:
        load.start()
    for load, store in zip(loads, stores):
        load.wait()
        store.start()
    for store in stores:
        store.wait()


def per_device(queries, key_tokens, value_tokens, grad_out, out_weight, pattern, valid_rows):
    count = lax.axis_size("lon")
    rows, features = queries.shape
    n_blocks = 2 * count
    pairs = features // PAIR
    shape = jax.ShapeDtypeStruct((rows, features), BF16)
    hbm = pl.BlockSpec(memory_space=pltpu.HBM)
    smem = pl.BlockSpec(memory_space=pltpu.SMEM)
    dma = pltpu.SemaphoreType.DMA
    outs = pl.pallas_call(
        functools.partial(kernel, count),
        out_shape=(shape,) * 4,
        in_specs=[smem, smem] + [hbm] * 5,
        out_specs=(hbm,) * 4,
        scratch_shapes=[
            pltpu.VMEM((rows, features), BF16),
            pltpu.VMEM((rows, features), BF16),
            pltpu.VMEM((rows, features), BF16),
            pltpu.VMEM((rows, features), BF16),
            pltpu.VMEM((features, features), BF16),
            pltpu.VMEM((rows, features), BF16),
            pltpu.VMEM((rows, features), BF16),
            pltpu.VMEM((rows, features), BF16),
            pltpu.VMEM((rows, features), BF16),
            dma((5,)),
            dma((2 + 2 * (features // GROUP),)),
            pltpu.VMEM((2, 2, rows, features), BF16),
            pltpu.VMEM((2, 2, rows, features), BF16),
            pltpu.VMEM((2, 2, rows, features), BF16),
            pltpu.VMEM((2, rows, features), F32),
            pltpu.VMEM((rows, features), BF16),
            pltpu.VMEM((rows, features), BF16),
            pltpu.VMEM((count, 16, GROUP), BF16),
            pltpu.VMEM((2, n_blocks, features), BF16),
            pltpu.VMEM((2, n_blocks, features), BF16),
            pltpu.VMEM((count, 16, GROUP), BF16),
            pltpu.VMEM((count, 16, GROUP), BF16),
            dma((2, 2, pairs)),
            dma((2, 2, pairs)),
            dma((2, 2, pairs)),
            dma((2, 2, pairs)),
            dma((count,)),
            dma((count,)),
            dma((count,)),
            dma((count,)),
        ],
        compiler_params=pltpu.CompilerParams(
            collective_id=0, has_side_effects=True, vmem_limit_bytes=63 * 2**20
        ),
        cost_estimate=pl.CostEstimate(
            flops=2_600_000_000, bytes_accessed=6_500_000, transcendentals=1_800_000
        ),
    )(pattern.T, valid_rows, queries, key_tokens, value_tokens, grad_out, out_weight)
    return pl.pallas_call(
        hand_over,
        out_shape=(shape,) * 4,
        in_specs=[hbm] * 4,
        out_specs=(hbm,) * 4,
        scratch_shapes=[pltpu.VMEM((4, rows, features), BF16), dma((4,)), dma((4,))],
    )(*outs)


def solution(mesh):
    split = P(("groups", "lon"), None)
    return jax.shard_map(
        per_device,
        mesh=mesh,
        in_specs=(split, split, split, split, P(), P(), P()),
        out_specs=(split,) * 4,
        check_vma=False,
    )
```

```python
import functools

import jax
import jax.numpy as jnp
from jax import lax
from jax.experimental import pallas as pl
from jax.experimental.pallas import tpu as pltpu
from jax.sharding import PartitionSpec as P

HEADS = 16
TILE = 128
PAIR = 128
GROUP = 256
BEFORE = 2
AHEAD = 4
SPLIT = 4
F32 = jnp.float32
BF16 = jnp.bfloat16


def nn(a, b):
    return lax.dot_general(a, b, (((1,), (0,)), ((), ())), preferred_element_type=F32)


def nt(a, b):
    return lax.dot_general(a, b, (((1,), (1,)), ((), ())), preferred_element_type=F32)


def tn(a, b):
    return lax.dot_general(a, b, (((0,), (0,)), ((), ())), preferred_element_type=F32)


def kernel(
    count,
    pattern, valid, queries_hbm, keys_hbm, values_hbm, grad_out_hbm, weight_hbm,
    layer_out_hbm, grad_queries_hbm, grad_keys_hbm, grad_values_hbm,
    queries, keys, values, grad_out, weight,
    layer_out, grad_queries, grad_keys, grad_values, load_sem, store_sem,
    halo, back_out, back_in, own, attended, grad_att,
    gathered, far_kv, far_sum, far_out, far_in,
    halo_send, halo_recv, back_send, back_recv,
    sum_send, sum_recv, far_send, far_recv,
):
    me = lax.axis_index("lon")
    east = lax.rem(me + 1, count)
    west = lax.rem(me + count - 1, count)
    rows, features = queries.shape
    pairs = features // PAIR
    groups = features // GROUP
    n_blocks = 2 * count
    kv_refs = (keys, values)
    sides = (west, east)

    def peer(step):
        return lax.rem(me + step, count)

    def source(step):
        return lax.rem(me + count - step, count)

    barrier = pltpu.get_barrier_semaphore()

    def greet(step, carry):
        pl.semaphore_signal(
            barrier, inc=1, device_id={"lon": peer(step)}, device_id_type=pl.DeviceIdType.MESH
        )
        return carry

    lax.fori_loop(1, count, greet, 0)
    loads = [
        pltpu.make_async_copy(far, near, load_sem.at[i])
        for i, (far, near) in enumerate(
            (
                (keys_hbm, keys),
                (values_hbm, values),
                (grad_out_hbm, grad_out),
                (weight_hbm, weight),
                (queries_hbm, queries),
            )
        )
    ]
    for load in loads:
        load.start()
    loads[0].wait()
    loads[1].wait()

    def columns(pair):
        return pl.ds(pl.multiple_of(pair * PAIR, PAIR), PAIR)

    def halo_copy(side, kind, pair):
        return pltpu.make_async_remote_copy(
            src_ref=kv_refs[kind].at[:, columns(pair)],
            dst_ref=halo.at[1 - side, kind, :, columns(pair)],
            send_sem=halo_send.at[side, kind, pair],
            recv_sem=halo_recv.at[1 - side, kind, pair],
            device_id={"lon": sides[side]},
            device_id_type=pl.DeviceIdType.MESH,
        )

    def halo_arrival(slot, kind, pair):
        return pltpu.make_async_remote_copy(
            src_ref=kv_refs[kind].at[:, columns(pair)],
            dst_ref=halo.at[slot, kind, :, columns(pair)],
            send_sem=halo_send.at[slot, kind, pair],
            recv_sem=halo_recv.at[slot, kind, pair],
            device_id={"lon": sides[slot]},
            device_id_type=pl.DeviceIdType.MESH,
        )

    def back_copy(side, kind, pair):
        return pltpu.make_async_remote_copy(
            src_ref=back_out.at[side, kind, :, columns(pair)],
            dst_ref=back_in.at[1 - side, kind, :, columns(pair)],
            send_sem=back_send.at[side, kind, pair],
            recv_sem=back_recv.at[1 - side, kind, pair],
            device_id={"lon": sides[side]},
            device_id_type=pl.DeviceIdType.MESH,
        )

    def back_arrival(slot, kind, pair):
        return pltpu.make_async_remote_copy(
            src_ref=back_out.at[slot, kind, :, columns(pair)],
            dst_ref=back_in.at[slot, kind, :, columns(pair)],
            send_sem=back_send.at[slot, kind, pair],
            recv_sem=back_recv.at[slot, kind, pair],
            device_id={"lon": sides[slot]},
            device_id_type=pl.DeviceIdType.MESH,
        )

    def summary_copy(step, slot):
        return pltpu.make_async_remote_copy(
            src_ref=gathered.at[slot],
            dst_ref=gathered.at[slot],
            send_sem=sum_send.at[step],
            recv_sem=sum_recv.at[step],
            device_id={"lon": peer(step)},
            device_id_type=pl.DeviceIdType.MESH,
        )

    def far_copy(step, taken, slot):
        return pltpu.make_async_remote_copy(
            src_ref=far_out.at[taken],
            dst_ref=far_in.at[slot],
            send_sem=far_send.at[step],
            recv_sem=far_recv.at[step],
            device_id={"lon": peer(step)},
            device_id_type=pl.DeviceIdType.MESH,
        )

    def send_halo(pair):
        for kind in range(2):
            for side in range(2):
                halo_copy(side, kind, pair).start()

    own_count = [valid[2 * me + b] for b in range(2)]
    root_row = lax.broadcasted_iota(jnp.int32, (16, GROUP), 0)
    root = jnp.sqrt(
        jnp.where(root_row % 2 == 0, own_count[0], own_count[1]).astype(F32)
    )
    pool_row = lax.broadcasted_iota(jnp.int32, (16, rows), 0)
    pool_col = lax.broadcasted_iota(jnp.int32, (16, rows), 1)
    pool_live = pool_col < jnp.where(pool_col < TILE, own_count[0], own_count[1] + TILE)
    pool_block = jnp.where(pool_col < TILE, 0, 1)
    pooled = jnp.zeros((16, GROUP), F32)
    for c in range(groups):
        for kind in range(2):
            chosen = (pool_row == 4 * c + 2 * kind + pool_block) & pool_live
            pooled += nn(
                chosen.astype(F32).astype(BF16), kv_refs[kind][:, c * GROUP : (c + 1) * GROUP]
            )
    gathered[me] = (pooled / root).astype(BF16)

    def send_summary(step, carry):
        summary_copy(step, me).start()
        return carry

    pl.semaphore_wait(barrier, count - 1)
    lax.fori_loop(1, count, send_summary, 0)
    for pair in range(BEFORE):
        send_halo(pair)

    for load in loads[2:]:
        load.wait()
    part = slice(0, GROUP)
    grad_att[:, part] = nt(grad_out[...], weight[part, :]).astype(BF16)

    def take_summary(step, carry):
        summary_copy(step, source(step)).wait_recv()
        return carry

    lax.fori_loop(1, count, take_summary, 0)
    for pair in range(BEFORE, AHEAD):
        send_halo(pair)
    for c in range(1, groups):
        part = slice(c * GROUP, (c + 1) * GROUP)
        grad_att[:, part] = nt(grad_out[...], weight[part, :]).astype(BF16)
    pieces = gathered[...].reshape(count * 16, GROUP)
    sel_row = lax.broadcasted_iota(jnp.int32, (n_blocks, count * 16), 0)
    sel_col = lax.broadcasted_iota(jnp.int32, (n_blocks, count * 16), 1)
    sel_place = (sel_row // 2) * 16 + sel_row % 2
    for c in range(groups):
        for kind in range(2):
            chosen = (sel_col == sel_place + (4 * c + 2 * kind)).astype(F32).astype(BF16)
            far_kv[kind, :, c * GROUP : (c + 1) * GROUP] = nn(chosen, pieces).astype(BF16)

    lane = lax.broadcasted_iota(jnp.int32, (1, PAIR), 1)
    first = (lane < PAIR // 2).astype(F32).astype(BF16)
    second = (lane >= PAIR // 2).astype(F32).astype(BF16)
    half = TILE // 2
    key_row = lax.broadcasted_iota(jnp.int32, (half, 2 * TILE), 0) + half
    block_info = []
    for b in range(2):
        west_block = pattern[0, 2 * me + b]
        east_block = pattern[2, 2 * me + b]
        picks = [(lax.rem(blk, 2) == 0) for blk in (west_block, east_block)]
        counts = (valid[west_block], own_count[b], valid[east_block])
        block_info.append((picks, counts))

    def heads_of(tensor):
        return jnp.concatenate((tensor * first, tensor * second), axis=0)

    def unfold(tensor):
        return jnp.concatenate(
            (tensor[: PAIR // 2, :TILE], tensor[PAIR // 2 :, TILE:]), axis=0
        ).T

    def step_pair(pair, carry):
        cols = columns(pair)

        @pl.when(pair + AHEAD < pairs)
        def _():
            send_halo(pair + AHEAD)

        for kind in range(2):
            for slot in range(2):
                halo_arrival(slot, kind, pair).wait_recv()

        edges = []
        far_total = [None, None]
        for b in range(2):
            picks, counts = block_info[b]
            band = pl.ds(b * TILE, TILE)
            sets = []
            for kind in range(2):
                near = []
                for slot in range(2):
                    near.append(
                        lax.select(
                            picks[slot],
                            halo[slot, kind, pl.ds(0, TILE), cols],
                            halo[slot, kind, pl.ds(TILE, TILE), cols],
                        )
                    )
                sets.append(
                    jnp.concatenate(
                        (near[0], kv_refs[kind][band, cols], near[1], far_kv[kind, :, cols]),
                        axis=0,
                    )
                )
            all_keys, all_values = sets
            query = heads_of(queries[band, cols] * jnp.asarray(0.125, BF16))
            grads = heads_of(grad_att[band, cols])
            scores = nt(all_keys, query)
            parts = []
            for slot in range(3):
                base = slot * TILE
                parts.append(scores[base : base + half])
                parts.append(
                    jnp.where(
                        key_row < counts[slot], scores[base + half : base + TILE], -jnp.inf
                    )
                )
            parts.append(scores[3 * TILE :])
            scores = jnp.concatenate(parts, axis=0)
            top = jnp.max(scores, axis=0, keepdims=True)
            weights = jnp.exp(scores - top)
            total = jnp.sum(weights, axis=0, keepdims=True)
            grad_chances = nt(all_values, grads)
            chances = weights * (1.0 / total)
            rounded = chances.astype(BF16)
            delta = jnp.sum(chances * grad_chances, axis=0, keepdims=True)
            grad_scores = (chances * (grad_chances - delta)).astype(BF16)
            attended[band, cols] = unfold(tn(all_values, rounded)).astype(BF16)
            grad_queries[band, cols] = (unfold(tn(all_keys, grad_scores)) * 0.125).astype(BF16)
            results = (nn(grad_scores, query), nn(rounded, grads))
            sides_of = []
            for kind in range(2):
                full = results[kind]
                own[kind, band, cols] = full[TILE : 2 * TILE]
                far = full[3 * TILE :]
                far_total[kind] = far if b == 0 else far_total[kind] + far
                sides_of.append((full[:TILE], full[2 * TILE : 3 * TILE]))
            edges.append(sides_of)

        for kind in range(2):
            far_sum[kind, :, cols] = far_total[kind].astype(BF16)
            for side in range(2):
                low = [jnp.where(block_info[b][0][side], 1.0, 0.0).astype(F32) for b in range(2)]
                one, two = edges[0][kind][side], edges[1][kind][side]
                back_out[side, kind, pl.ds(0, TILE), cols] = (
                    one * low[0] + two * low[1]
                ).astype(BF16)
                back_out[side, kind, pl.ds(TILE, TILE), cols] = (
                    one * (1.0 - low[0]) + two * (1.0 - low[1])
                ).astype(BF16)
        for kind in range(2):
            for side in range(2):
                back_copy(side, kind, pair).start()
        return carry

    lax.fori_loop(0, pairs, step_pair, 0)

    put_row = lax.broadcasted_iota(jnp.int32, (count * 16, n_blocks), 0)
    put_col = lax.broadcasted_iota(jnp.int32, (count * 16, n_blocks), 1)
    put_place = (put_col // 2) * 16 + put_col % 2
    packed = jnp.zeros((count * 16, GROUP), F32)
    for c in range(groups):
        for kind in range(2):
            chosen = (put_row == put_place + (4 * c + 2 * kind)).astype(F32).astype(BF16)
            packed += nn(chosen, far_sum[kind, :, c * GROUP : (c + 1) * GROUP])
    far_out[...] = packed.astype(BF16).reshape(count, 16, GROUP)
    far_in[me] = far_out[me]

    def send_far(step, carry):
        far_copy(step, peer(step), me).start()
        return carry

    lax.fori_loop(1, count, send_far, 0)

    for c in range(groups):
        part = slice(c * GROUP, (c + 1) * GROUP)
        layer_out[:, part] = nn(attended[...], weight[:, part]).astype(BF16)
    stores = [
        pltpu.make_async_copy(layer_out, layer_out_hbm, store_sem.at[0]),
        pltpu.make_async_copy(grad_queries, grad_queries_hbm, store_sem.at[1]),
    ]
    for store in stores:
        store.start()

    def take_far(step, carry):
        far_copy(step, peer(step), source(step)).wait_recv()
        return carry

    lax.fori_loop(1, count, take_far, 0)
    spread = jnp.sum(far_in[...].astype(F32), axis=0) / root
    live_row = lax.broadcasted_iota(jnp.int32, (TILE, GROUP), 0)
    outs = (grad_keys, grad_values)
    outs_hbm = (grad_keys_hbm, grad_values_hbm)
    for c in range(groups):
        part = slice(c * GROUP, (c + 1) * GROUP)
        for pair in range(c * GROUP // PAIR, (c + 1) * GROUP // PAIR):
            for kind in range(2):
                for slot in range(2):
                    back_arrival(slot, kind, pair).wait_recv()
        for kind in range(2):
            for b in range(2):
                band = slice(b * TILE, (b + 1) * TILE)
                line = 4 * c + 2 * kind + b
                far = jnp.where(live_row < own_count[b], spread[line : line + 1, :], 0.0)
                outs[kind][band, part] = (
                    own[kind, band, part]
                    + back_in[0, kind, band, part].astype(F32)
                    + back_in[1, kind, band, part].astype(F32)
                    + far
                ).astype(BF16)
            store = pltpu.make_async_copy(
                outs[kind].at[:, part], outs_hbm[kind].at[:, part], store_sem.at[2 + 2 * c + kind]
            )
            store.start()
            stores.append(store)

    def drain_pair(pair, carry):
        for kind in range(2):
            for side in range(2):
                halo_copy(side, kind, pair).wait_send()
                back_copy(side, kind, pair).wait_send()
        return carry

    lax.fori_loop(0, pairs, drain_pair, 0)

    def drain_peer(step, carry):
        summary_copy(step, me).wait_send()
        far_copy(step, peer(step), me).wait_send()
        return carry

    lax.fori_loop(1, count, drain_peer, 0)
    for store in stores:
        store.wait()


def hand_over(*refs):
    sources, targets, buffers, load_sem, store_sem = refs[:4], refs[4:8], refs[8], refs[9], refs[10]
    size = buffers.shape[1] // SPLIT
    loads, stores = [], []
    for n in range(4 * SPLIT):
        i, band = n // SPLIT, pl.ds(n % SPLIT * size, size)
        loads.append(
            pltpu.make_async_copy(sources[i].at[band], buffers.at[i, band], load_sem.at[n])
        )
        stores.append(
            pltpu.make_async_copy(buffers.at[i, band], targets[i].at[band], store_sem.at[n])
        )
    for load in loads:
        load.start()
    for load, store in zip(loads, stores):
        load.wait()
        store.start()
    for store in stores:
        store.wait()


def per_device(queries, key_tokens, value_tokens, grad_out, out_weight, pattern, valid_rows):
    count = lax.axis_size("lon")
    rows, features = queries.shape
    n_blocks = 2 * count
    pairs = features // PAIR
    shape = jax.ShapeDtypeStruct((rows, features), BF16)
    hbm = pl.BlockSpec(memory_space=pltpu.HBM)
    smem = pl.BlockSpec(memory_space=pltpu.SMEM)
    dma = pltpu.SemaphoreType.DMA
    outs = pl.pallas_call(
        functools.partial(kernel, count),
        out_shape=(shape,) * 4,
        in_specs=[smem, smem] + [hbm] * 5,
        out_specs=(hbm,) * 4,
        scratch_shapes=[
            pltpu.VMEM((rows, features), BF16),
            pltpu.VMEM((rows, features), BF16),
            pltpu.VMEM((rows, features), BF16),
            pltpu.VMEM((rows, features), BF16),
            pltpu.VMEM((features, features), BF16),
            pltpu.VMEM((rows, features), BF16),
            pltpu.VMEM((rows, features), BF16),
            pltpu.VMEM((rows, features), BF16),
            pltpu.VMEM((rows, features), BF16),
            dma((5,)),
            dma((2 + 2 * (features // GROUP),)),
            pltpu.VMEM((2, 2, rows, features), BF16),
            pltpu.VMEM((2, 2, rows, features), BF16),
            pltpu.VMEM((2, 2, rows, features), BF16),
            pltpu.VMEM((2, rows, features), F32),
            pltpu.VMEM((rows, features), BF16),
            pltpu.VMEM((rows, features), BF16),
            pltpu.VMEM((count, 16, GROUP), BF16),
            pltpu.VMEM((2, n_blocks, features), BF16),
            pltpu.VMEM((2, n_blocks, features), BF16),
            pltpu.VMEM((count, 16, GROUP), BF16),
            pltpu.VMEM((count, 16, GROUP), BF16),
            dma((2, 2, pairs)),
            dma((2, 2, pairs)),
            dma((2, 2, pairs)),
            dma((2, 2, pairs)),
            dma((count,)),
            dma((count,)),
            dma((count,)),
            dma((count,)),
        ],
        compiler_params=pltpu.CompilerParams(
            collective_id=0, has_side_effects=True, vmem_limit_bytes=63 * 2**20
        ),
        cost_estimate=pl.CostEstimate(
            flops=2_600_000_000, bytes_accessed=6_500_000, transcendentals=1_800_000
        ),
    )(pattern.T, valid_rows, queries, key_tokens, value_tokens, grad_out, out_weight)
    return pl.pallas_call(
        hand_over,
        out_shape=(shape,) * 4,
        in_specs=[hbm] * 4,
        out_specs=(hbm,) * 4,
        scratch_shapes=[
            pltpu.VMEM((4, rows, features), BF16), dma((4 * SPLIT,)), dma((4 * SPLIT,))
        ],
    )(*outs)


def solution(mesh):
    split = P(("groups", "lon"), None)
    return jax.shard_map(
        per_device,
        mesh=mesh,
        in_specs=(split, split, split, split, P(), P(), P()),
        out_specs=(split,) * 4,
        check_vma=False,
    )
```
